32 devices in a mesh: rep: 2 (over y), store: 4 (over z), tp: 4 (over x, core).
Axes of the slice: x: 2, y: 2, z: 4, core: 2. Of those that a mesh axis runs over, the one named last changes fastest.
Arguments:
- tokens: bfloat16 [384, 5120], P(('rep', 'store'), 'tp'), parts along dimension 0, may hold values from -6 to 6
- gate_weight: bfloat16 [5120, 16384], P('tp', 'store'), may hold values from -0.078125 to 0.078125
- up_weight: bfloat16 [5120, 16384], P('tp', 'store'), may hold values from -0.078125 to 0.078125
- down_weight: bfloat16 [16384, 5120], P('store', 'tp'), may hold values from -0.046875 to 0.046875
- factor_a: bfloat16 [128, 32, 5120], P(('rep', 'store'), None, 'tp'), parts along dimension 0, may hold values from -0.078125 to 0.078125
- factor_b: bfloat16 [128, 32, 16384], P(('rep', 'tp'), None, 'store'), parts along dimension 0, may hold values from -1.5 to 1.5
- adapter_slot: int32 [128], P('rep'), parts along dimension 0, may hold values from 0 to 63, as said below
- seg_adapter: int32 [8, 24], P(('rep', 'store')), parts along dimension 0, may hold values from 0 to 63, as said below
- row_segment: int32 [8, 48], P(('rep', 'store')), parts along dimension 0, may hold values from 0 to 23, never falling along the last dimension, each value on 1 to 4 neighbouring positions
Outputs:
- layer_out: bfloat16 [384, 5120], P(('rep', 'store'), 'tp'), parts along dimension 0
The draws below stay inside these ranges and needn't reach their ends.
There are 2 independent parts, one for each index of `rep`. The reference program is written for one: setup_inputs(seed, part) draws one part's arguments, and reference() takes and returns one part's arrays. A program takes and returns all parts, laid end to end along the dimension named above; an argument that names none is the same for every part. Nothing has to cross between parts.
Inputs may be any that keep to these rules, and one draw needn't show every extreme that they name: A permutation: adapter a lies in row adapter_slot[a] of factor_a and factor_b; rows g * 16 up to (g + 1) * 16 belong to store index g. `seg_adapter`: the 24 segments of one store index name distinct adapters; at most 6 of them lie in the rows of one store index, and for every store index some store index holds exactly 6 of its segments' adapters.
All inputs are finite; a program needn't handle non-finite values.
Results may differ from the reference program's by a relative error of at most 0.02.
Values may be sent and summed in bfloat16 or wider, within the bound.
A program may use at most 128 MiB of HBM per device.

```python
import math
import jax
import jax.numpy as jnp
import numpy as np
from jax import lax

D = 5120
FF = 16384
R = 16
NSEG = 24
TOK_DEV = 48
ADP_DEV = 16
ADAPTERS = 64
CAP = 6
TOKENS = 192
N_STORE = 4
N_TP = 4


def stored_rows(key):
    return jax.random.permutation(jax.random.fold_in(key, 17), ADAPTERS).astype(jnp.int32)


def group_rows(key):
    keys = jax.random.split(key, 4)
    first_owner = jax.random.randint(keys[0], (), 0, N_STORE)
    others = jax.random.permutation(keys[1], (N_STORE - 1) * CAP)[:NSEG - CAP]
    owner_ids = jnp.concatenate([jnp.full((CAP,), first_owner, jnp.int32), ((others // CAP + first_owner + 1) % N_STORE).astype(jnp.int32)])
    rank_ids = jnp.concatenate([jnp.arange(CAP, dtype=jnp.int32), (others % CAP).astype(jnp.int32)])
    offsets = jax.random.randint(keys[2], (N_STORE,), 0, ADP_DEV)
    local_ids = (offsets[owner_ids] + rank_ids) % ADP_DEV
    table_rows = owner_ids * ADP_DEV + local_ids
    return table_rows[jax.random.permutation(keys[3], NSEG)].astype(jnp.int32)


def draw_adapter_slot(key, part):
    table = stored_rows(key)
    return table


def draw_seg_adapter(key, part):
    table = stored_rows(key)
    key = jax.random.fold_in(key, 5)
    rows = jax.vmap(group_rows)(jax.random.split(key, N_STORE))
    inverse = jnp.argsort(table).astype(jnp.int32)
    return inverse[rows].astype(jnp.int32)


def levels(rng, shape, shards, smallest, largest):
    factor_of, own = 1.0, jax.random.fold_in(rng, 6)
    for dim, shards_of in shards:
        steps = jnp.exp(jax.random.uniform(jax.random.fold_in(own, dim), (shards_of,), jnp.float32, smallest / len(shards), largest / len(shards)))
        factor_of = factor_of * jnp.repeat(steps, shape[dim] // shards_of).reshape([-1 if axis == dim else 1 for axis in range(len(shape))])
    return factor_of


def length_profile(number_of, total, limit, lean):
    portions = [(1 << 20) // math.isqrt(grade ** lean) + 1 for grade in range(2, number_of + 1)]
    rest, given = total - limit - (number_of - 1), [1] * (number_of - 1)
    while rest > 0:
        candidates = [i for i in range(number_of - 1) if given[i] < limit]
        whole, budget = sum([portions[i] for i in candidates]), rest
        for i in candidates:
            addition = min(limit - given[i], max(1, budget * portions[i] // whole), rest)
            given[i] = given[i] + addition
            rest = rest - addition
    return np.array([limit] + given)


def ragged(own_key, number_of, total, reach, slope):
    if number_of == 2:
        one = jax.random.randint(own_key, (), max(1, total - reach), min(reach, total - 1) + 1)
        return jnp.stack([one, total - one])
    sizes = jnp.asarray(length_profile(number_of, total, reach, slope), jnp.int32)
    couples = (number_of - 1) // 2
    giver, taker = sizes[1:1 + 2 * couples:2], sizes[2:2 + 2 * couples:2]
    room = jnp.minimum(giver - 1, reach - taker)
    shifted = jax.random.randint(jax.random.fold_in(own_key, 1), (couples,), 0, 1 << 20) % (room + 1)
    sizes = sizes.at[1:1 + 2 * couples:2].set(giver - shifted).at[2:2 + 2 * couples:2].set(taker + shifted)
    return sizes[jax.random.permutation(jax.random.fold_in(own_key, 2), number_of)]


def bell_draw(key, extent, scale, reach, pieces=(), kind=jnp.bfloat16):
    level = levels(key, extent, pieces, -0.22, 0.18) if pieces else 1.0
    entries = jax.random.normal(key, extent, jnp.float32) * scale * level
    return jnp.minimum(jnp.maximum(entries, -reach), reach).astype(kind)


def setup_inputs(seed: int = 0, part: int = 0) -> dict:
    streams_of = jax.random.split(jax.random.key(seed), 10)
    own_keys = jax.random.split(jax.random.fold_in(streams_of[9], part), 10)
    return {
        "tokens": bell_draw(own_keys[0], (TOKENS, D), 1.0, 6.0, ((0, 4), (1, 4))),
        "gate_weight": bell_draw(streams_of[1], (D, FF), D ** -0.5, 0.078125, ((0, 4), (1, 4))),
        "up_weight": bell_draw(streams_of[2], (D, FF), D ** -0.5, 0.078125, ((0, 4), (1, 4))),
        "down_weight": bell_draw(streams_of[3], (FF, D), FF ** -0.5, 0.046875, ((0, 4), (1, 4))),
        "factor_a": bell_draw(own_keys[4], (ADAPTERS, 2 * R, D), D ** -0.5, 0.078125, ((0, 4), (2, 4))),
        "factor_b": bell_draw(own_keys[5], (ADAPTERS, 2 * R, FF), R ** -0.5, 1.5, ((0, 4), (2, 4))),
        "adapter_slot": draw_adapter_slot(jax.random.fold_in(jax.random.fold_in(streams_of[9], part), 71), part),
        "seg_adapter": draw_seg_adapter(jax.random.fold_in(jax.random.fold_in(streams_of[9], part), 71), part),
        "row_segment": jax.vmap(lambda own: jnp.searchsorted(jnp.cumsum(ragged(own, NSEG, TOK_DEV, 2 * TOK_DEV // NSEG, 2)), jnp.arange(TOK_DEV), side="right"))(jax.random.split(own_keys[8], N_STORE)).reshape((N_STORE, TOK_DEV)).astype(jnp.int32),
    }


def round_trip(values):
    return lax.optimization_barrier(values.astype(jnp.bfloat16)).astype(values.dtype)


def reference(tokens, gate_weight, up_weight, down_weight, factor_a, factor_b, adapter_slot, seg_adapter, row_segment):
    seg_rows = adapter_slot[seg_adapter].astype(jnp.int32)
    token_rows = jnp.take_along_axis(seg_rows, row_segment, axis=1).astype(jnp.int32)
    grouped = tokens.reshape(N_STORE, TOK_DEV, D)

    def group_terms(batch):
        row_ids, group_tok = batch
        a_rows = factor_a[row_ids].astype(jnp.float32)
        low_rank = jnp.einsum("td,tkd->tk", group_tok.astype(jnp.float32), a_rows)
        low_wide = round_trip(low_rank)
        b_rows = factor_b[row_ids].astype(jnp.float32)
        extra_gate = jnp.einsum("tk,tkf->tf", low_wide[:, :R], b_rows[:, :R])
        extra_up = jnp.einsum("tk,tkf->tf", low_wide[:, R:], b_rows[:, R:])
        return extra_gate, extra_up

    extra_gate, extra_up = lax.map(group_terms, (token_rows, grouped))
    extra_gate = extra_gate.reshape(TOKENS, FF)
    extra_up = extra_up.reshape(TOKENS, FF)
    lanes = token_rows.reshape(TOKENS) // (ADAPTERS // N_TP)
    width = D // N_TP

    def tp_step(carry, lane):
        gate_sum, up_sum = carry
        columns = lax.dynamic_slice_in_dim(tokens, lane * width, width, 1)
        gate_rows = lax.dynamic_slice_in_dim(gate_weight, lane * width, width, 0)
        up_rows = lax.dynamic_slice_in_dim(up_weight, lane * width, width, 0)
        chosen = (lanes == lane)[:, None]
        gate_part = jnp.dot(columns, gate_rows, preferred_element_type=jnp.float32) + jnp.where(chosen, extra_gate, 0.0)
        up_part = jnp.dot(columns, up_rows, preferred_element_type=jnp.float32) + jnp.where(chosen, extra_up, 0.0)
        return (gate_sum + round_trip(gate_part), up_sum + round_trip(up_part)), None

    zeros_ff = jnp.zeros((TOKENS, FF), jnp.float32)
    (gate_sum, up_sum), _ = lax.scan(tp_step, (zeros_ff, zeros_ff), jnp.arange(N_TP, dtype=jnp.int32))
    hidden = (jax.nn.silu(gate_sum) * up_sum).astype(jnp.bfloat16)
    block = FF // N_STORE

    def store_step(total, index):
        hidden_cols = lax.dynamic_slice_in_dim(hidden, index * block, block, 1)
        down_rows = lax.dynamic_slice_in_dim(down_weight, index * block, block, 0)
        return total + round_trip(jnp.dot(hidden_cols, down_rows, preferred_element_type=jnp.float32)), None

    total, _ = lax.scan(store_step, jnp.zeros((TOKENS, D), jnp.float32), jnp.arange(N_STORE, dtype=jnp.int32))
    return total.astype(jnp.bfloat16)
```

```python
import functools
import jax
import jax.numpy as jnp
from jax import lax
from jax.experimental import pallas as pl
from jax.experimental.pallas import tpu as pltpu
from jax.sharding import PartitionSpec as P

MESH = pl.DeviceIdType.MESH
CHUNK = 256
SPLIT = (32, 16)
LAGS = (1, 2, 3, 4)
F32 = jnp.float32
BF16 = jnp.bfloat16


def lookup_table(table_vals, id_vals):
    hit_mask = id_vals[..., None] == jnp.arange(table_vals.shape[0], dtype=jnp.int32)
    return jnp.sum(jnp.where(hit_mask, table_vals, 0), axis=-1)


def body(
    tokens,
    gate_weight,
    up_weight,
    down_weight,
    factor_a,
    factor_b,
    adapter_slot,
    seg_adapter,
    row_segment,
):
    tok_dev = tokens.shape[0]
    d_loc = tokens.shape[1]
    ff_loc = gate_weight.shape[1]
    rank_both = factor_a.shape[1]
    rank_width = rank_both // 2
    adapter_rows = factor_a.shape[0]
    block_rows = factor_b.shape[0]
    nseg = seg_adapter.shape[1]
    store_count = lax.axis_size("store")
    store_index = lax.axis_index("store")
    tp_index = lax.axis_index("tp")
    total_rows = tok_dev * store_count
    seg_lists, row_lists = (
        lax.all_gather(seg_adapter, "store", axis=0, tiled=True),
        lax.all_gather(row_segment, "store", axis=0, tiled=True),
    )
    seg_rows = lookup_table(adapter_slot, seg_lists)
    seg_match = row_lists[..., None] == jnp.arange(nseg, dtype=jnp.int32)
    token_rows = jnp.sum(jnp.where(seg_match, seg_rows[:, None, :], 0), axis=-1).reshape(total_rows)
    piece_rows = lax.all_gather(tokens, "store", axis=0, tiled=True)
    projected = jnp.concatenate(
        [
            jnp.dot(piece_rows, gate_weight, preferred_element_type=jnp.float32),
            jnp.dot(piece_rows, up_weight, preferred_element_type=jnp.float32),
        ],
        axis=1,
    )
    capacity = max(2, nseg // store_count)
    owner_ids = seg_rows // adapter_rows
    local_ids = seg_rows % adapter_rows
    same_owner = owner_ids[:, :, None] == owner_ids[:, None, :]
    before = jnp.arange(nseg)[None, :] < jnp.arange(nseg)[:, None]
    rank_ids = jnp.sum(same_owner & before[None], axis=2)
    to_me = owner_ids == store_index
    wanted = to_me[:, :, None] & (rank_ids[:, :, None] == jnp.arange(capacity, dtype=jnp.int32))
    send_local = jnp.sum(jnp.where(wanted, local_ids[:, :, None], 0), axis=1)
    blocks = jnp.take(factor_a, send_local.reshape(-1), axis=0).reshape(
        store_count, capacity, rank_both, d_loc
    )
    received = lax.all_to_all(blocks, "store", split_axis=0, concat_axis=0, tiled=True)
    home_owner = lax.dynamic_index_in_dim(owner_ids, store_index, 0, keepdims=False)
    home_rank = lax.dynamic_index_in_dim(rank_ids, store_index, 0, keepdims=False)
    pick_index = home_owner * capacity + home_rank
    seg_blocks = jnp.take(
        received.reshape(store_count * capacity, rank_both, d_loc), pick_index, axis=0
    )
    scores = jnp.einsum("td,skd->tsk", tokens, seg_blocks, preferred_element_type=jnp.float32)
    local_mask = row_segment[0][:, None] == jnp.arange(nseg, dtype=jnp.int32)
    partial_value = jnp.sum(jnp.where(local_mask[:, :, None], scores, 0.0), axis=1)
    home_low = lax.psum(partial_value, "tp")
    low_rank = lax.all_gather(home_low, "store", axis=0, tiled=True)
    low_half = low_rank.astype(jnp.bfloat16)
    in_block = token_rows[:, None] == tp_index * block_rows + jnp.arange(
        block_rows, dtype=jnp.int32
    )

    def spread_rows(factor_half):
        placed = jnp.where(
            in_block[:, :, None], factor_half[:, None, :], jnp.zeros((), jnp.bfloat16)
        )
        return placed.reshape(total_rows, block_rows * rank_width)

    b_gate = factor_b[:, :rank_width, :].reshape(block_rows * rank_width, ff_loc)
    b_up = factor_b[:, rank_width:, :].reshape(block_rows * rank_width, ff_loc)
    gate_part = projected[:, :ff_loc] + jnp.dot(
        spread_rows(low_half[:, :rank_width]), b_gate, preferred_element_type=jnp.float32
    )
    up_part = projected[:, ff_loc:] + jnp.dot(
        spread_rows(low_half[:, rank_width:]), b_up, preferred_element_type=jnp.float32
    )
    gate_sum, up_sum = (
        lax.psum(gate_part.astype(jnp.bfloat16), "tp").astype(jnp.float32),
        lax.psum(up_part.astype(jnp.bfloat16), "tp").astype(jnp.float32),
    )
    hidden = (jax.nn.silu(gate_sum) * up_sum).astype(jnp.bfloat16)
    return lax.psum_scatter(
        jnp.dot(hidden, down_weight, preferred_element_type=jnp.float32).astype(jnp.bfloat16),
        "store",
        scatter_dimension=0,
        tiled=True,
    )


def dot(left, right, contract=(1, 0)):
    dims = (((contract[0],), (contract[1],)), ((), ()))
    return lax.dot_general(left, right, dims, preferred_element_type=F32)


def fused_kernel(
    tok_ref, gate_ref, up_ref, down_ref, fa_ref, fb_ref, slot_ref, seg_ref, row_ref,
    out_ref,
    meta, tok_a, tok_b, fa, w_buf, b_buf, d_buf,
    low_send_a, low_send_b, low_recv_a, low_recv_b, spread_a, spread_b,
    sib_send_a, sib_send_b, sib_recv_a, sib_recv_b, keep_a, keep_b,
    x_send_a, x_send_b, x_recv_a, x_recv_b, hid_a, hid_b, acc_a, acc_b,
    z_send_a, z_send_b, z_recv_a, z_recv_b,
    load_w, load_b, load_d, load_fa,
    meta_s, meta_r, tok_s, tok_r, low_s, low_r, sib_s, sib_r, x_s, x_r,
    hx_s, hx_r, h1_s, h1_r, h3_s, h3_r, z_s, z_r,
):
    stores = lax.axis_size("store")
    s = lax.axis_index("store")
    t = lax.axis_index("tp")
    core = lax.rem(t, 2)
    sib = t + 1 - 2 * core
    opp = lax.rem(t + 2, 4)
    diag = lax.rem(sib + 2, 4)
    rows_of = fa_ref.shape[0]
    ff_loc, width = down_ref.shape
    quarter = ff_loc // 4
    w = CHUNK
    chunks = quarter // w
    toks, low_sends, low_recvs = (tok_a, tok_b), (low_send_a, low_send_b), (low_recv_a, low_recv_b)
    spreads = (spread_a, spread_b)
    sib_sends, sib_recvs, keeps = (sib_send_a, sib_send_b), (sib_recv_a, sib_recv_b), (keep_a, keep_b)
    x_sends, x_recvs, hids, accs = (x_send_a, x_send_b), (x_recv_a, x_recv_b), (hid_a, hid_b), (acc_a, acc_b)
    z_sends, z_recvs = (z_send_a, z_send_b), (z_recv_a, z_recv_b)
    starts = (0, SPLIT[0])
    pending = []

    def remote(src, dst, send_sem, recv_sem, **where):
        return pltpu.make_async_remote_copy(
            src_ref=src, dst_ref=dst, send_sem=send_sem, recv_sem=recv_sem,
            device_id=where, device_id_type=MESH,
        )

    load_a = pltpu.make_async_copy(fa_ref, fa, load_fa)
    load_a.start()
    owners = ((lax.rem(sib + 2, 4), sib), (opp, t))
    w_loads, b_loads, d_loads = {}, {}, {}
    for c in range(chunks):
        for h in range(2):
            for j in range(4):
                col = pl.multiple_of(owners[h][j % 2] * quarter + c * w, w)
                ref = gate_ref if j < 2 else up_ref
                cp = pltpu.make_async_copy(
                    ref.at[:, pl.ds(col, w)], w_buf.at[c, h, j], load_w.at[c, h, j])
                cp.start()
                w_loads[c, h, j] = cp
                half = fb_ref.shape[1] // 2
                cb = pltpu.make_async_copy(
                    fb_ref.at[:, pl.ds((j // 2) * half, half), pl.ds(col, w)],
                    b_buf.at[c, h, j], load_b.at[c, h, j])
                cb.start()
                b_loads[c, h, j] = cb
    for c in range(chunks):
        for q, owner in enumerate((t, sib, opp, diag)):
            row = pl.multiple_of(owner * quarter + c * w, w)
            cp = pltpu.make_async_copy(
                down_ref.at[pl.ds(row, w), :], d_buf.at[c, pl.ds(q * w, w), :], load_d.at[c, q])
            cp.start()
            d_loads[c, q] = cp

    bar = pltpu.get_barrier_semaphore()
    pl.semaphore_signal(bar, inc=1, device_id={"tp": sib}, device_id_type=MESH)
    pl.semaphore_signal(bar, inc=1, device_id={"tp": opp}, device_id_type=MESH)
    for d in range(1, stores):
        pl.semaphore_signal(
            bar, inc=1, device_id={"store": lax.rem(s + d, stores)}, device_id_type=MESH)
    for u in range(4):
        @pl.when(jnp.logical_not(jnp.logical_and(s == t, t == u)))
        def _():
            pl.semaphore_signal(bar, inc=1, device_id={"store": t, "tp": u}, device_id_type=MESH)
    meta[s, 0:1, 0:seg_ref.shape[1]] = seg_ref[...]
    meta[s, 1:2, 0:row_ref.shape[1]] = row_ref[...]
    pl.semaphore_wait(bar, 2 + (stores - 1) + 4 - jnp.where(s == t, 1, 0))

    meta_copies, tok_copies = [], {}
    for d in range(1, stores):
        peer = lax.rem(s + d, stores)
        cp = remote(meta.at[s], meta.at[s], meta_s.at[d - 1], meta_r.at[d - 1], store=peer)
        cp.start()
        meta_copies.append(cp)
    for r in range(2):
        n = SPLIT[r]
        for d in range(1, stores):
            peer = lax.rem(s + d, stores)
            cp = remote(
                tok_ref.at[pl.ds(starts[r], n), :],
                toks[r].at[pl.ds(pl.multiple_of(s * n, n), n), :],
                tok_s.at[r, d - 1], tok_r.at[r, d - 1], store=peer)
            cp.start()
            tok_copies[r, d] = cp
        toks[r][pl.ds(pl.multiple_of(s * n, n), n), :] = tok_ref[pl.ds(starts[r], n), :]
    for cp in meta_copies:
        cp.wait_recv()
    pending += meta_copies + list(tok_copies.values())

    per = tok_ref.shape[0]
    lane = lax.broadcasted_iota(jnp.int32, (per, 128), 1)
    sub = lax.broadcasted_iota(jnp.int32, (per, 128), 0)
    slots = slot_ref[...].astype(F32)
    n_slot = slots.shape[1]
    lane_slot = lax.broadcasted_iota(jnp.int32, (per, n_slot), 1).astype(F32)
    lane_f = lane.astype(F32)
    table = []
    for g in range(stores):
        segs = meta[g, 0:1, :].astype(F32)
        belongs = meta[g, 1:2, :].astype(F32)
        seg_col = jnp.sum(jnp.where(lane == sub, belongs, 0.0), axis=1, keepdims=True)
        adp_col = jnp.sum(jnp.where(lane_f == seg_col, segs, 0.0), axis=1, keepdims=True)
        table.append(jnp.sum(jnp.where(lane_slot == adp_col, slots, 0.0), axis=1, keepdims=True))
    rows_at = []
    for r in range(2):
        n = SPLIT[r]
        m = n * stores
        lane_m = lax.broadcasted_iota(jnp.int32, (per, m), 1)
        sub_m = lax.broadcasted_iota(jnp.int32, (per, m), 0)
        total = jnp.zeros((1, m), F32)
        for g in range(stores):
            hit = lane_m == sub_m - starts[r] + g * n
            inside = jnp.logical_and(sub_m >= starts[r], sub_m < starts[r] + n)
            total += jnp.sum(
                jnp.where(jnp.logical_and(hit, inside), table[g], 0.0), axis=0, keepdims=True)
        rows_at.append(total)

    rank2 = fa_ref.shape[1]
    low_copies = {}

    def low_start(r):
        for d in range(1, stores):
            tok_copies[r, d].wait_recv()
        if r == 0:
            load_a.wait()
        scores = dot(fa[...].reshape(rows_of * rank2, width), toks[r][...], (1, 1))
        mine = jnp.zeros((rank2, scores.shape[1]), F32)
        for a in range(rows_of):
            here = rows_at[r] == (s * rows_of + a).astype(F32)
            mine += jnp.where(here, scores[a * rank2:(a + 1) * rank2, :], 0.0)
        low_sends[r][...] = mine
        for g in range(stores):
            cp = remote(
                low_sends[r], low_recvs[r].at[t], low_s.at[r, g], low_r.at[r, t], store=g, tp=s)
            own = jnp.logical_and(s == t, s == g)
            low_copies[r, g] = cp

            @pl.when(jnp.logical_not(own))
            def _():
                cp.start()

            @pl.when(own)
            def _():
                low_recvs[r][t] = mine

    def low_finish(r):
        for u in range(4):
            @pl.when(jnp.logical_not(jnp.logical_and(s == t, t == u)))
            def _():
                remote(low_sends[r], low_recvs[r].at[u], low_s.at[r, 0], low_r.at[r, u],
                       store=t, tp=u).wait_recv()
        total = low_recvs[r][0] + low_recvs[r][1] + low_recvs[r][2] + low_recvs[r][3]
        total = total.astype(BF16).astype(F32)
        half = rank2 // 2
        for gu in range(2):
            piece = total[gu * half:(gu + 1) * half, :]
            placed = jnp.concatenate(
                [
                    jnp.where(rows_at[r] == (t * rows_of + a).astype(F32), piece, 0.0)
                    for a in range(rows_of)
                ],
                axis=0,
            )
            spreads[r][gu] = placed.T.astype(BF16)

    def term(r, c, h, j):
        b = b_buf[c, h, j].reshape(spreads[r].shape[2], w)
        return dot(toks[r][...], w_buf[c, h, j]) + dot(spreads[r][j // 2], b)

    sib_copies, x_copies, hx_copies, h1_copies, h3_copies, z_copies = {}, {}, {}, {}, {}, {}

    def phase1(r, c):
        if r == 0:
            for j in range(4):
                w_loads[c, 0, j].wait()
                b_loads[c, 0, j].wait()

        @pl.loop(0, 4)
        def _(j):
            sib_sends[r][c, j] = term(r, c, 0, j).astype(BF16)

        cp = remote(sib_sends[r].at[c], sib_recvs[r].at[c], sib_s.at[r, c], sib_r.at[r, c], tp=sib)
        cp.start()
        sib_copies[r, c] = cp
        if r == 0:
            for j in range(4):
                w_loads[c, 1, j].wait()
                b_loads[c, 1, j].wait()

        @pl.loop(0, 4)
        def _(j):
            keeps[r][c, j] = term(r, c, 1, j)

    def phase2(r, c):
        sib_copies[r, c].wait_recv()
        for gu in range(2):
            x_sends[r][c, gu] = (
                keeps[r][c, 2 * gu] + sib_recvs[r][c, 2 * gu].astype(F32)).astype(BF16)
        cp = remote(x_sends[r].at[c], x_recvs[r].at[c], x_s.at[r, c], x_r.at[r, c], tp=opp)
        cp.start()
        x_copies[r, c] = cp
        for gu in range(2):
            keeps[r][c, 2 * gu + 1] += sib_recvs[r][c, 2 * gu + 1].astype(F32)

    def phase3(r, c):
        x_copies[r, c].wait_recv()
        gate = keeps[r][c, 1] + x_recvs[r][c, 0].astype(F32)
        up = keeps[r][c, 3] + x_recvs[r][c, 1].astype(F32)
        hids[r][c, :, 0:w] = (gate / (1.0 + jnp.exp(-gate)) * up).astype(BF16)
        mine = hids[r].at[c, :, pl.ds(0, w)]
        cp = remote(mine, hids[r].at[c, :, pl.ds(2 * w, w)], hx_s.at[r, c], hx_r.at[r, c], tp=opp)
        cp.start()
        hx_copies[r, c] = cp
        cp = remote(mine, hids[r].at[c, :, pl.ds(w, w)], h1_s.at[r, c], h1_r.at[r, c], tp=sib)
        cp.start()
        h1_copies[r, c] = cp

    def phase4(r, c):
        hx_copies[r, c].wait_recv()
        cp = remote(
            hids[r].at[c, :, pl.ds(2 * w, w)], hids[r].at[c, :, pl.ds(3 * w, w)],
            h3_s.at[r, c], h3_r.at[r, c], tp=sib)
        cp.start()
        h3_copies[r, c] = cp

    def phase5(r, c):
        h1_copies[r, c].wait_recv()
        h3_copies[r, c].wait_recv()
        if r == 0:
            for q in range(4):
                d_loads[c, q].wait()
        n = SPLIT[r]
        tile = 256
        for lo in range(0, width, tile):
            value = dot(hids[r][c], d_buf[c, :, lo:lo + tile])
            if c > 0:
                value += accs[r][:, lo:lo + tile]
            if c < chunks - 1:
                accs[r][:, lo:lo + tile] = value
            else:
                z_sends[r][:, lo:lo + tile] = value.astype(BF16)
        if c == chunks - 1:
            for d in range(1, stores):
                peer = lax.rem(s + d, stores)
                cp = remote(
                    z_sends[r].at[pl.ds(pl.multiple_of(peer * n, n), n), :],
                    z_recvs[r].at[d - 1], z_s.at[r, d - 1], z_r.at[r, d - 1], store=peer)
                cp.start()
                z_copies[r, d] = cp

    order = [(r, c) for r in range(2) for c in range(chunks)]
    phases = (phase2, phase3, phase4, phase5)
    low_start(0)
    low_finish(0)
    for k in range(len(order) + LAGS[-1]):
        if k == 2:
            low_start(1)
        if k == chunks:
            low_finish(1)
        if k < len(order):
            phase1(*order[k])
        for lag, phase in zip(LAGS, phases):
            if 0 <= k - lag < len(order):
                phase(*order[k - lag])
    for r in range(2):
        n = SPLIT[r]
        total = z_sends[r][pl.ds(pl.multiple_of(s * n, n), n), :].astype(F32)
        for d in range(1, stores):
            z_copies[r, d].wait_recv()
            total += z_recvs[r][d - 1].astype(F32)
        out_ref[starts[r]:starts[r] + n, :] = total.astype(BF16)
    for group in (sib_copies, x_copies, hx_copies, h1_copies, h3_copies, z_copies):
        pending += list(group.values())
    for cp in pending:
        cp.wait_send()
    for (r, g), cp in low_copies.items():
        @pl.when(jnp.logical_not(jnp.logical_and(s == t, s == g)))
        def _():
            cp.wait_send()


def fused_body(
    tokens, gate_weight, up_weight, down_weight, factor_a, factor_b,
    adapter_slot, seg_adapter, row_segment,
):
    stores = lax.axis_size("store")
    ff_loc, width = down_weight.shape
    w = CHUNK
    chunks = ff_loc // 4 // w
    rows_of, rank2, _ = factor_a.shape
    half = rank2 // 2
    m = tuple(n * stores for n in SPLIT)

    def both(shape_of, kind):
        return [pltpu.VMEM(shape_of(r), kind) for r in range(2)]

    dma = pltpu.SemaphoreType.DMA
    scratch = [
        pltpu.VMEM((stores, 8, 128), jnp.int32),
        *both(lambda r: (m[r], width), BF16),
        pltpu.VMEM(factor_a.shape, BF16),
        pltpu.VMEM((chunks, 2, 4, width, w), BF16),
        pltpu.VMEM((chunks, 2, 4, rows_of, half, w), BF16),
        pltpu.VMEM((chunks, 4 * w, width), BF16),
        *both(lambda r: (rank2, m[r]), F32),
        *both(lambda r: (4, rank2, m[r]), F32),
        *both(lambda r: (2, m[r], rows_of * half), BF16),
        *both(lambda r: (chunks, 4, m[r], w), BF16),
        *both(lambda r: (chunks, 4, m[r], w), BF16),
        *both(lambda r: (chunks, 4, m[r], w), F32),
        *both(lambda r: (chunks, 2, m[r], w), BF16),
        *both(lambda r: (chunks, 2, m[r], w), BF16),
        *both(lambda r: (chunks, m[r], 4 * w), BF16),
        *both(lambda r: (m[r], width), F32),
        *both(lambda r: (m[r], width), BF16),
        *both(lambda r: (stores - 1, SPLIT[r], width), BF16),
        dma((chunks, 2, 4)), dma((chunks, 2, 4)), dma((chunks, 4)), dma,
        dma((stores - 1,)), dma((stores - 1,)),
        dma((2, stores - 1)), dma((2, stores - 1)),
        dma((2, stores)), dma((2, 4)),
        *[dma((2, chunks)) for _ in range(10)],
        dma((2, stores - 1)), dma((2, stores - 1)),
    ]
    vmem = pl.BlockSpec(memory_space=pltpu.VMEM)
    hbm = pl.BlockSpec(memory_space=pl.ANY)
    return pl.pallas_call(
        fused_kernel,
        out_shape=jax.ShapeDtypeStruct(tokens.shape, BF16),
        in_specs=[vmem, hbm, hbm, hbm, hbm, hbm, vmem, vmem, vmem],
        out_specs=vmem,
        scratch_shapes=scratch,
        compiler_params=pltpu.CompilerParams(
            collective_id=0, has_side_effects=True, vmem_limit_bytes=60 * 1024 * 1024
        ),
    )(
        tokens, gate_weight, up_weight, down_weight, factor_a, factor_b,
        adapter_slot.reshape(1, -1), seg_adapter, row_segment,
    )


def solution(mesh):
    placed = (
        P(("rep", "store"), "tp"),
        P("tp", "store"),
        P("tp", "store"),
        P("store", "tp"),
        P(("rep", "store"), None, "tp"),
        P(("rep", "tp"), None, "store"),
        P("rep"),
        P(("rep", "store"), None),
        P(("rep", "store"), None),
    )
    fused = mesh.shape["store"] == 4 and mesh.shape["tp"] == 4
    return jax.shard_map(
        fused_body if fused else body, mesh=mesh, in_specs=placed, out_specs=P(("rep", "store"), "tp"), check_vma=False
    )
```

```python
import functools
import jax
import jax.numpy as jnp
from jax import lax
from jax.experimental import pallas as pl
from jax.experimental.pallas import tpu as pltpu
from jax.sharding import PartitionSpec as P

MESH = pl.DeviceIdType.MESH
CHUNK = 256
SPLIT = (32, 16)
LAGS = (1, 3, 5, 6)
EARLY = 1
F32 = jnp.float32
BF16 = jnp.bfloat16


def lookup_table(table_vals, id_vals):
    hit_mask = id_vals[..., None] == jnp.arange(table_vals.shape[0], dtype=jnp.int32)
    return jnp.sum(jnp.where(hit_mask, table_vals, 0), axis=-1)


def body(
    tokens,
    gate_weight,
    up_weight,
    down_weight,
    factor_a,
    factor_b,
    adapter_slot,
    seg_adapter,
    row_segment,
):
    tok_dev = tokens.shape[0]
    d_loc = tokens.shape[1]
    ff_loc = gate_weight.shape[1]
    rank_both = factor_a.shape[1]
    rank_width = rank_both // 2
    adapter_rows = factor_a.shape[0]
    block_rows = factor_b.shape[0]
    nseg = seg_adapter.shape[1]
    store_count = lax.axis_size("store")
    store_index = lax.axis_index("store")
    tp_index = lax.axis_index("tp")
    total_rows = tok_dev * store_count
    seg_lists, row_lists = (
        lax.all_gather(seg_adapter, "store", axis=0, tiled=True),
        lax.all_gather(row_segment, "store", axis=0, tiled=True),
    )
    seg_rows = lookup_table(adapter_slot, seg_lists)
    seg_match = row_lists[..., None] == jnp.arange(nseg, dtype=jnp.int32)
    token_rows = jnp.sum(jnp.where(seg_match, seg_rows[:, None, :], 0), axis=-1).reshape(total_rows)
    piece_rows = lax.all_gather(tokens, "store", axis=0, tiled=True)
    projected = jnp.concatenate(
        [
            jnp.dot(piece_rows, gate_weight, preferred_element_type=jnp.float32),
            jnp.dot(piece_rows, up_weight, preferred_element_type=jnp.float32),
        ],
        axis=1,
    )
    capacity = max(2, nseg // store_count)
    owner_ids = seg_rows // adapter_rows
    local_ids = seg_rows % adapter_rows
    same_owner = owner_ids[:, :, None] == owner_ids[:, None, :]
    before = jnp.arange(nseg)[None, :] < jnp.arange(nseg)[:, None]
    rank_ids = jnp.sum(same_owner & before[None], axis=2)
    to_me = owner_ids == store_index
    wanted = to_me[:, :, None] & (rank_ids[:, :, None] == jnp.arange(capacity, dtype=jnp.int32))
    send_local = jnp.sum(jnp.where(wanted, local_ids[:, :, None], 0), axis=1)
    blocks = jnp.take(factor_a, send_local.reshape(-1), axis=0).reshape(
        store_count, capacity, rank_both, d_loc
    )
    received = lax.all_to_all(blocks, "store", split_axis=0, concat_axis=0, tiled=True)
    home_owner = lax.dynamic_index_in_dim(owner_ids, store_index, 0, keepdims=False)
    home_rank = lax.dynamic_index_in_dim(rank_ids, store_index, 0, keepdims=False)
    pick_index = home_owner * capacity + home_rank
    seg_blocks = jnp.take(
        received.reshape(store_count * capacity, rank_both, d_loc), pick_index, axis=0
    )
    scores = jnp.einsum("td,skd->tsk", tokens, seg_blocks, preferred_element_type=jnp.float32)
    local_mask = row_segment[0][:, None] == jnp.arange(nseg, dtype=jnp.int32)
    partial_value = jnp.sum(jnp.where(local_mask[:, :, None], scores, 0.0), axis=1)
    home_low = lax.psum(partial_value, "tp")
    low_rank = lax.all_gather(home_low, "store", axis=0, tiled=True)
    low_half = low_rank.astype(jnp.bfloat16)
    in_block = token_rows[:, None] == tp_index * block_rows + jnp.arange(
        block_rows, dtype=jnp.int32
    )

    def spread_rows(factor_half):
        placed = jnp.where(
            in_block[:, :, None], factor_half[:, None, :], jnp.zeros((), jnp.bfloat16)
        )
        return placed.reshape(total_rows, block_rows * rank_width)

    b_gate = factor_b[:, :rank_width, :].reshape(block_rows * rank_width, ff_loc)
    b_up = factor_b[:, rank_width:, :].reshape(block_rows * rank_width, ff_loc)
    gate_part = projected[:, :ff_loc] + jnp.dot(
        spread_rows(low_half[:, :rank_width]), b_gate, preferred_element_type=jnp.float32
    )
    up_part = projected[:, ff_loc:] + jnp.dot(
        spread_rows(low_half[:, rank_width:]), b_up, preferred_element_type=jnp.float32
    )
    gate_sum, up_sum = (
        lax.psum(gate_part.astype(jnp.bfloat16), "tp").astype(jnp.float32),
        lax.psum(up_part.astype(jnp.bfloat16), "tp").astype(jnp.float32),
    )
    hidden = (jax.nn.silu(gate_sum) * up_sum).astype(jnp.bfloat16)
    return lax.psum_scatter(
        jnp.dot(hidden, down_weight, preferred_element_type=jnp.float32).astype(jnp.bfloat16),
        "store",
        scatter_dimension=0,
        tiled=True,
    )


def dot(left, right, contract=(1, 0)):
    dims = (((contract[0],), (contract[1],)), ((), ()))
    return lax.dot_general(left, right, dims, preferred_element_type=F32)


def fused_kernel(
    tok_ref, gate_ref, up_ref, down_ref, fa_ref, fb_ref, slot_ref, seg_ref, row_ref,
    out_ref,
    meta, toks, fa, w_buf, b_buf, d_buf, low_sends, low_recvs, spreads,
    sib_sends, sib_recvs, keeps, x_sends, x_recvs, hids, accs, z_sends, z_recvs,
    load_w, load_b, load_d, load_fa,
    meta_s, meta_r, tok_s, tok_r, low_s, low_r, sib_s, sib_r, x_s, x_r,
    hx_s, hx_r, h1_s, h1_r, h3_s, h3_r, z_s, z_r,
):
    stores = lax.axis_size("store")
    s = lax.axis_index("store")
    t = lax.axis_index("tp")
    core = lax.rem(t, 2)
    sib = t + 1 - 2 * core
    opp = lax.rem(t + 2, 4)
    diag = lax.rem(sib + 2, 4)
    rows_of = fa_ref.shape[0]
    ff_loc, width = down_ref.shape
    quarter = ff_loc // 4
    w = CHUNK
    chunks = quarter // w
    blocks = len(SPLIT)
    starts = tuple(sum(SPLIT[:r]) for r in range(blocks))
    pending = []

    def remote(src, dst, send_sem, recv_sem, **where):
        return pltpu.make_async_remote_copy(
            src_ref=src, dst_ref=dst, send_sem=send_sem, recv_sem=recv_sem,
            device_id=where, device_id_type=MESH,
        )

    load_a = pltpu.make_async_copy(fa_ref, fa, load_fa)
    load_a.start()
    owners = ((lax.rem(sib + 2, 4), sib), (opp, t))
    w_loads, b_loads, d_loads = {}, {}, {}

    def load_columns(c):
        half = fb_ref.shape[1] // 2
        for h in range(2):
            for j in range(4):
                col = pl.multiple_of(owners[h][j % 2] * quarter + c * w, w)
                ref = gate_ref if j < 2 else up_ref
                cp = pltpu.make_async_copy(
                    ref.at[:, pl.ds(col, w)], w_buf.at[c, h, j], load_w.at[c, h, j])
                cp.start()
                w_loads[c, h, j] = cp
                cb = pltpu.make_async_copy(
                    fb_ref.at[:, pl.ds((j // 2) * half, half), pl.ds(col, w)],
                    b_buf.at[c, h, j], load_b.at[c, h, j])
                cb.start()
                b_loads[c, h, j] = cb

    def load_down(c):
        for q, owner in enumerate((t, sib, opp, diag)):
            row = pl.multiple_of(owner * quarter + c * w, w)
            cp = pltpu.make_async_copy(
                down_ref.at[pl.ds(row, w), :], d_buf.at[c, pl.ds(q * w, w), :], load_d.at[c, q])
            cp.start()
            d_loads[c, q] = cp

    for c in range(EARLY):
        load_columns(c)

    bar = pltpu.get_barrier_semaphore()
    pl.semaphore_signal(bar, inc=1, device_id={"tp": sib}, device_id_type=MESH)
    pl.semaphore_signal(bar, inc=1, device_id={"tp": opp}, device_id_type=MESH)
    for d in range(1, stores):
        pl.semaphore_signal(
            bar, inc=1, device_id={"store": lax.rem(s + d, stores)}, device_id_type=MESH)
    for u in range(4):
        @pl.when(jnp.logical_not(jnp.logical_and(s == t, t == u)))
        def _():
            pl.semaphore_signal(bar, inc=1, device_id={"store": t, "tp": u}, device_id_type=MESH)
    meta[s, 0:1, 0:seg_ref.shape[1]] = seg_ref[...]
    meta[s, 1:2, 0:row_ref.shape[1]] = row_ref[...]
    pl.semaphore_wait(bar, 2 + (stores - 1) + 4 - jnp.where(s == t, 1, 0))

    meta_copies, tok_copies = [], {}
    for d in range(1, stores):
        peer = lax.rem(s + d, stores)
        cp = remote(meta.at[s], meta.at[s], meta_s.at[d - 1], meta_r.at[d - 1], store=peer)
        cp.start()
        meta_copies.append(cp)
    for r in range(blocks):
        n = SPLIT[r]
        for d in range(1, stores):
            peer = lax.rem(s + d, stores)
            cp = remote(
                tok_ref.at[pl.ds(starts[r], n), :],
                toks[r].at[pl.ds(pl.multiple_of(s * n, n), n), :],
                tok_s.at[r, d - 1], tok_r.at[r, d - 1], store=peer)
            cp.start()
            tok_copies[r, d] = cp
        toks[r][pl.ds(pl.multiple_of(s * n, n), n), :] = tok_ref[pl.ds(starts[r], n), :]
    for c in range(EARLY, chunks):
        load_columns(c)
    for c in range(chunks):
        load_down(c)
    for cp in meta_copies:
        cp.wait_recv()
    pending += meta_copies + list(tok_copies.values())

    per = tok_ref.shape[0]
    lane = lax.broadcasted_iota(jnp.int32, (per, 128), 1)
    sub = lax.broadcasted_iota(jnp.int32, (per, 128), 0)
    slots = slot_ref[...].astype(F32)
    n_slot = slots.shape[1]
    lane_slot = lax.broadcasted_iota(jnp.int32, (per, n_slot), 1).astype(F32)
    lane_f = lane.astype(F32)
    table = []
    for g in range(stores):
        segs = meta[g, 0:1, :].astype(F32)
        belongs = meta[g, 1:2, :].astype(F32)
        seg_col = jnp.sum(jnp.where(lane == sub, belongs, 0.0), axis=1, keepdims=True)
        adp_col = jnp.sum(jnp.where(lane_f == seg_col, segs, 0.0), axis=1, keepdims=True)
        table.append(jnp.sum(jnp.where(lane_slot == adp_col, slots, 0.0), axis=1, keepdims=True))
    rows_at = []
    for r in range(blocks):
        n = SPLIT[r]
        m = n * stores
        lane_m = lax.broadcasted_iota(jnp.int32, (per, m), 1)
        sub_m = lax.broadcasted_iota(jnp.int32, (per, m), 0)
        total = jnp.zeros((1, m), F32)
        for g in range(stores):
            hit = lane_m == sub_m - starts[r] + g * n
            inside = jnp.logical_and(sub_m >= starts[r], sub_m < starts[r] + n)
            total += jnp.sum(
                jnp.where(jnp.logical_and(hit, inside), table[g], 0.0), axis=0, keepdims=True)
        rows_at.append(total)

    rank2 = fa_ref.shape[1]
    low_copies = {}

    def low_start(r):
        for d in range(1, stores):
            tok_copies[r, d].wait_recv()
        if r == 0:
            load_a.wait()
        scores = dot(fa[...].reshape(rows_of * rank2, width), toks[r][...], (1, 1))
        mine = jnp.zeros((rank2, scores.shape[1]), F32)
        for a in range(rows_of):
            here = rows_at[r] == (s * rows_of + a).astype(F32)
            mine += jnp.where(here, scores[a * rank2:(a + 1) * rank2, :], 0.0)
        low_sends[r][...] = mine
        for g in range(stores):
            cp = remote(
                low_sends[r], low_recvs[r].at[t], low_s.at[r, g], low_r.at[r, t], store=g, tp=s)
            own = jnp.logical_and(s == t, s == g)
            low_copies[r, g] = cp

            @pl.when(jnp.logical_not(own))
            def _():
                cp.start()

            @pl.when(own)
            def _():
                low_recvs[r][t] = mine

    def low_finish(r):
        for u in range(4):
            @pl.when(jnp.logical_not(jnp.logical_and(s == t, t == u)))
            def _():
                remote(low_sends[r], low_recvs[r].at[u], low_s.at[r, 0], low_r.at[r, u],
                       store=t, tp=u).wait_recv()
        total = low_recvs[r][0] + low_recvs[r][1] + low_recvs[r][2] + low_recvs[r][3]
        total = total.astype(BF16).astype(F32)
        half = rank2 // 2
        for gu in range(2):
            piece = total[gu * half:(gu + 1) * half, :]
            placed = jnp.concatenate(
                [
                    jnp.where(rows_at[r] == (t * rows_of + a).astype(F32), piece, 0.0)
                    for a in range(rows_of)
                ],
                axis=0,
            )
            spreads[r][gu] = placed.T.astype(BF16)

    def term(r, c, h, j):
        b = b_buf[c, h, j].reshape(spreads[r].shape[2], w)
        return dot(toks[r][...], w_buf[c, h, j]) + dot(spreads[r][j // 2], b)

    sib_copies, x_copies, hx_copies, h1_copies, h3_copies, z_copies = {}, {}, {}, {}, {}, {}

    def phase1(r, c):
        if r == 0:
            for j in range(4):
                w_loads[c, 0, j].wait()
                b_loads[c, 0, j].wait()

        @pl.loop(0, 4)
        def _(j):
            sib_sends[r][c, j] = term(r, c, 0, j).astype(BF16)

        cp = remote(sib_sends[r].at[c], sib_recvs[r].at[c], sib_s.at[r, c], sib_r.at[r, c], tp=sib)
        cp.start()
        sib_copies[r, c] = cp
        if r == 0:
            for j in range(4):
                w_loads[c, 1, j].wait()
                b_loads[c, 1, j].wait()

        @pl.loop(0, 4)
        def _(j):
            keeps[r][c, j] = term(r, c, 1, j)

    def phase2(r, c):
        sib_copies[r, c].wait_recv()
        for gu in range(2):
            x_sends[r][c, gu] = (
                keeps[r][c, 2 * gu] + sib_recvs[r][c, 2 * gu].astype(F32)).astype(BF16)
        cp = remote(x_sends[r].at[c], x_recvs[r].at[c], x_s.at[r, c], x_r.at[r, c], tp=opp)
        cp.start()
        x_copies[r, c] = cp
        for gu in range(2):
            keeps[r][c, 2 * gu + 1] += sib_recvs[r][c, 2 * gu + 1].astype(F32)

    def phase3(r, c):
        x_copies[r, c].wait_recv()
        gate = keeps[r][c, 1] + x_recvs[r][c, 0].astype(F32)
        up = keeps[r][c, 3] + x_recvs[r][c, 1].astype(F32)
        hids[r][c, :, 0:w] = (gate / (1.0 + jnp.exp(-gate)) * up).astype(BF16)
        mine = hids[r].at[c, :, pl.ds(0, w)]
        cp = remote(mine, hids[r].at[c, :, pl.ds(2 * w, w)], hx_s.at[r, c], hx_r.at[r, c], tp=opp)
        cp.start()
        hx_copies[r, c] = cp
        cp = remote(mine, hids[r].at[c, :, pl.ds(w, w)], h1_s.at[r, c], h1_r.at[r, c], tp=sib)
        cp.start()
        h1_copies[r, c] = cp

    def phase4(r, c):
        hx_copies[r, c].wait_recv()
        cp = remote(
            hids[r].at[c, :, pl.ds(2 * w, w)], hids[r].at[c, :, pl.ds(3 * w, w)],
            h3_s.at[r, c], h3_r.at[r, c], tp=sib)
        cp.start()
        h3_copies[r, c] = cp

    def phase5(r, c):
        h1_copies[r, c].wait_recv()
        h3_copies[r, c].wait_recv()
        if r == 0:
            for q in range(4):
                d_loads[c, q].wait()
        n = SPLIT[r]
        tile = 256
        for lo in range(0, width, tile):
            value = dot(hids[r][c], d_buf[c, :, lo:lo + tile])
            if c > 0:
                value += accs[r][:, lo:lo + tile]
            if c < chunks - 1:
                accs[r][:, lo:lo + tile] = value
            else:
                z_sends[r][:, lo:lo + tile] = value.astype(BF16)
        if c == chunks - 1:
            for d in range(1, stores):
                peer = lax.rem(s + d, stores)
                cp = remote(
                    z_sends[r].at[pl.ds(pl.multiple_of(peer * n, n), n), :],
                    z_recvs[r].at[d - 1], z_s.at[r, d - 1], z_r.at[r, d - 1], store=peer)
                cp.start()
                z_copies[r, d] = cp

    order = [(r, c) for r in range(blocks) for c in range(chunks)]
    phases = (phase2, phase3, phase4, phase5)
    low_start(0)
    low_finish(0)
    for k in range(len(order) + LAGS[-1]):
        for r in range(1, blocks):
            if k == r * chunks - 2:
                low_start(r)
            if k == r * chunks:
                low_finish(r)
        if k < len(order):
            phase1(*order[k])
        for lag, phase in zip(LAGS, phases):
            if 0 <= k - lag < len(order):
                phase(*order[k - lag])
    for r in range(blocks):
        n = SPLIT[r]
        total = z_sends[r][pl.ds(pl.multiple_of(s * n, n), n), :].astype(F32)
        for d in range(1, stores):
            z_copies[r, d].wait_recv()
            total += z_recvs[r][d - 1].astype(F32)
        out_ref[starts[r]:starts[r] + n, :] = total.astype(BF16)
    for group in (sib_copies, x_copies, hx_copies, h1_copies, h3_copies, z_copies):
        pending += list(group.values())
    for cp in pending:
        cp.wait_send()
    for (r, g), cp in low_copies.items():
        @pl.when(jnp.logical_not(jnp.logical_and(s == t, s == g)))
        def _():
            cp.wait_send()


def fused_body(
    tokens, gate_weight, up_weight, down_weight, factor_a, factor_b,
    adapter_slot, seg_adapter, row_segment,
):
    stores = lax.axis_size("store")
    ff_loc, width = down_weight.shape
    w = CHUNK
    chunks = ff_loc // 4 // w
    rows_of, rank2, _ = factor_a.shape
    half = rank2 // 2
    m = tuple(n * stores for n in SPLIT)

    blocks = len(SPLIT)

    def each(shape_of, kind):
        return [pltpu.VMEM(shape_of(r), kind) for r in range(blocks)]

    dma = pltpu.SemaphoreType.DMA
    scratch = [
        pltpu.VMEM((stores, 8, 128), jnp.int32),
        each(lambda r: (m[r], width), BF16),
        pltpu.VMEM(factor_a.shape, BF16),
        pltpu.VMEM((chunks, 2, 4, width, w), BF16),
        pltpu.VMEM((chunks, 2, 4, rows_of, half, w), BF16),
        pltpu.VMEM((chunks, 4 * w, width), BF16),
        each(lambda r: (rank2, m[r]), F32),
        each(lambda r: (4, rank2, m[r]), F32),
        each(lambda r: (2, m[r], rows_of * half), BF16),
        each(lambda r: (chunks, 4, m[r], w), BF16),
        each(lambda r: (chunks, 4, m[r], w), BF16),
        each(lambda r: (chunks, 4, m[r], w), F32),
        each(lambda r: (chunks, 2, m[r], w), BF16),
        each(lambda r: (chunks, 2, m[r], w), BF16),
        each(lambda r: (chunks, m[r], 4 * w), BF16),
        each(lambda r: (m[r], width), F32),
        each(lambda r: (m[r], width), BF16),
        each(lambda r: (stores - 1, SPLIT[r], width), BF16),
        dma((chunks, 2, 4)), dma((chunks, 2, 4)), dma((chunks, 4)), dma,
        dma((stores - 1,)), dma((stores - 1,)),
        dma((blocks, stores - 1)), dma((blocks, stores - 1)),
        dma((blocks, stores)), dma((blocks, 4)),
        *[dma((blocks, chunks)) for _ in range(10)],
        dma((blocks, stores - 1)), dma((blocks, stores - 1)),
    ]
    vmem = pl.BlockSpec(memory_space=pltpu.VMEM)
    hbm = pl.BlockSpec(memory_space=pl.ANY)
    return pl.pallas_call(
        fused_kernel,
        out_shape=jax.ShapeDtypeStruct(tokens.shape, BF16),
        in_specs=[vmem, hbm, hbm, hbm, hbm, hbm, vmem, vmem, vmem],
        out_specs=vmem,
        scratch_shapes=scratch,
        compiler_params=pltpu.CompilerParams(
            collective_id=0, has_side_effects=True, vmem_limit_bytes=60 * 1024 * 1024
        ),
    )(
        tokens, gate_weight, up_weight, down_weight, factor_a, factor_b,
        adapter_slot.reshape(1, -1), seg_adapter, row_segment,
    )


def solution(mesh):
    placed = (
        P(("rep", "store"), "tp"),
        P("tp", "store"),
        P("tp", "store"),
        P("store", "tp"),
        P(("rep", "store"), None, "tp"),
        P(("rep", "tp"), None, "store"),
        P("rep"),
        P(("rep", "store"), None),
        P(("rep", "store"), None),
    )
    fused = mesh.shape["store"] == 4 and mesh.shape["tp"] == 4
    return jax.shard_map(
        fused_body if fused else body, mesh=mesh, in_specs=placed, out_specs=P(("rep", "store"), "tp"), check_vma=False
    )
```
